512 devices in a mesh: row: 16 (over y, x_hi), col: 32 (over x_lo, z, core).
Axes of the slice: x: 4 (x_hi: 2, x_lo: 2; x = x_hi * 2 + x_lo), y: 8, z: 8, core: 2. Of those that a mesh axis runs over, the one named last changes fastest.
Arguments:
- integrals: bfloat16 [800, 800, 640], P('row', 'col'), may hold values from -0.625 to 0.625
- amplitudes: bfloat16 [1024, 640], P('row', 'col'), may hold values from -6 to 6
- virt_irrep: int32 [800], replicated, may hold values from 0 to 7, as said below
- pair_irrep: int32 [640], replicated, may hold values from 0 to 7, as said below
- virt_energy: float32 [800], replicated, may hold values from 0.3 to 4
- occ_energy: float32 [32], replicated, may hold values from -2 to -0.3
Outputs:
- update: bfloat16 [800, 800, 1024], P('row', 'col')
The draws below stay inside these ranges and needn't reach their ends.
Inputs may be any that keep to these rules, and one draw needn't show every extreme that they name: `virt_irrep`: labels never fall along the index; each of the 8 labels covers one contiguous run of at least 66 orbitals. `pair_irrep`: labels never fall along the index; each of the 8 labels covers one contiguous run of at least 53 pairs.
All inputs are finite; a program needn't handle non-finite values.
Results may differ from the reference program's by a relative error of at most 0.0049.
Values may be sent and summed in bfloat16 or wider, within the bound.
A program may use at most 64 MiB of HBM per device.

```python
import math
import jax
import jax.numpy as jnp
from jax import lax

VIRT = 800
OCC = 32
CD = 640
PAIRS = 1024


def blocked_labels(key, total):
    least = total // 12
    spare = total - 8 * least
    labels = jnp.arange(8, dtype=jnp.int32)
    picks = jax.random.randint(key, (spare,), 0, 8)
    counts = least + jnp.sum((picks[:, None] == labels[None, :]).astype(jnp.int32), axis=0)
    ends = jnp.cumsum(counts).astype(jnp.int32)
    position = jnp.arange(total, dtype=jnp.int32)
    return jnp.sum((position[:, None] >= ends[None, :7]).astype(jnp.int32), axis=1).astype(jnp.int32)


def draw_virt_irrep(key, part):
    return blocked_labels(jax.random.fold_in(key, 11), VIRT)


def draw_pair_irrep(key, part):
    return blocked_labels(jax.random.fold_in(key, 23), CD)


def level_of(key, dims, cuts, smallest, high):
    gain = 1.0
    for axis_at, parts in cuts:
        steps = jax.random.uniform(jax.random.fold_in(jax.random.fold_in(key, 6), axis_at), (parts,), jnp.float32, smallest / len(cuts), high / len(cuts))
        gain = gain * jnp.repeat(jnp.exp(steps), dims[axis_at] // parts).reshape((-1,) + (1,) * (len(dims) - 1 - axis_at))
    return gain


def normal_values(key, extent, spread, reach, pieces=(), kind=jnp.bfloat16):
    drawn = jax.random.normal(key, extent, jnp.float32) * spread
    if len(pieces) > 0:
        drawn = level_of(key, extent, pieces, -0.22, 0.18) * drawn
    return jnp.clip(drawn, min=-reach, max=reach).astype(kind)


def setup_inputs(seed: int = 0) -> dict:
    splits = jax.random.split(jax.random.key(seed), 7)
    integrals = normal_values(splits[0], (VIRT, VIRT, CD), (CD // 8) ** -0.5, 0.625, ((0, 16), (1, 32)))
    amplitudes = normal_values(splits[1], (PAIRS, CD), 1.0, 6.0, ((0, 16), (1, 32)))
    virt_irrep = draw_virt_irrep(jax.random.fold_in(splits[6], 71), 0)
    pair_irrep = draw_pair_irrep(jax.random.fold_in(splits[6], 71), 0)
    virt_energy = jnp.clip(jnp.exp(jax.random.uniform(splits[4], (VIRT,), jnp.float32, math.log(0.3), math.log(4.0))), 0.3, 4.0)
    occ_energy = jnp.clip(jax.random.uniform(splits[5], (OCC,), jnp.float32, -2.0, -0.3), -2.0, -0.3)
    return dict(integrals=integrals, amplitudes=amplitudes, virt_irrep=virt_irrep, pair_irrep=pair_irrep, virt_energy=virt_energy, occ_energy=occ_energy)


def reference(integrals, amplitudes, virt_irrep, pair_irrep, virt_energy, occ_energy):
    width = VIRT // 16
    index = jnp.arange(16, dtype=jnp.int32)

    def contract(block):
        rows = lax.dynamic_slice_in_dim(integrals, block * width, width, 0)
        labels = lax.dynamic_slice_in_dim(virt_irrep, block * width, width, 0)
        keep = jnp.bitwise_xor(labels[:, None, None], virt_irrep[None, :, None]) == pair_irrep[None, None, :]
        masked = jnp.where(keep, rows, jnp.zeros((), rows.dtype))
        total = lax.dot_general(masked.reshape(width * VIRT, CD), amplitudes, (((1,), (1,)), ((), ())), preferred_element_type=jnp.float32)
        return total.astype(jnp.bfloat16).reshape(width, VIRT, PAIRS)

    ladder = lax.map(contract, index).reshape(VIRT, VIRT, PAIRS)
    pair_energy = (occ_energy[:, None] + occ_energy[None, :]).reshape(PAIRS)

    def finish(block):
        own = lax.dynamic_slice_in_dim(ladder, block * width, width, 0)
        other = lax.dynamic_slice_in_dim(ladder, block * width, width, 1)
        other = jnp.transpose(other.reshape(VIRT, width, OCC, OCC), (1, 0, 3, 2)).reshape(width, VIRT, PAIRS)
        first = lax.dynamic_slice_in_dim(virt_energy, block * width, width, 0)
        denom = first[:, None, None] + virt_energy[None, :, None] - pair_energy[None, None, :]
        return ((own.astype(jnp.float32) + other.astype(jnp.float32)) / denom).astype(jnp.bfloat16)

    return lax.map(finish, index).reshape(VIRT, VIRT, PAIRS)
```

```python
import functools

import jax
import jax.numpy as jnp
import numpy as np
from jax import lax
from jax.experimental import pallas as pl
from jax.experimental.pallas import tpu as pltpu
from jax.sharding import PartitionSpec as P

MESH = pl.DeviceIdType.MESH
BF = jnp.bfloat16
F32 = jnp.float32
I32 = jnp.int32
WIDE = 128
PIECES = 8
PIECE = 80
DETOURS = ((0, 0), (1, 1), (3, 7), (2, 2), (2, 6), (3, 3), (1, 5), (0, 4))


def pair_swapper(occupied):
    pairs = occupied * occupied
    source = jnp.arange(pairs, dtype=jnp.int32)
    target = source % occupied * occupied + source // occupied
    return (source[:, None] == target[None, :]).astype(jnp.bfloat16)


def long_runs(integrals, amplitudes, virt_irrep, pair_irrep, virt_energy, occ_energy):
    tile_a, tile_b, slab = integrals.shape
    occupied = occ_energy.shape[0]
    pairs = occupied * occupied
    row_at = lax.axis_index("row")
    col_at = lax.axis_index("col")
    labels_a = lax.dynamic_slice_in_dim(virt_irrep, row_at * tile_a, tile_a, 0)
    labels_b = lax.dynamic_slice_in_dim(virt_irrep, col_at * tile_b, tile_b, 0)
    keep = (
        jnp.bitwise_xor(labels_a[:, None, None], labels_b[None, :, None])
        == pair_irrep[None, None, :]
    )
    masked = jnp.where(keep, integrals, jnp.zeros((), integrals.dtype))
    flat = masked.reshape(tile_a * tile_b, slab)
    swapper = pair_swapper(occupied)
    all_pairs = lax.all_gather(amplitudes, "row", axis=0, tiled=True)
    totals = lax.dot_general(
        flat,
        lax.all_gather(all_pairs, "col", axis=1, tiled=True),
        (((1,), (1,)), ((), ())),
        preferred_element_type=jnp.float32,
    )
    rounded = totals.astype(jnp.bfloat16)
    ladder = rounded.reshape(tile_a, tile_b, pairs)
    first_move = lax.all_to_all(ladder, "row", split_axis=2, concat_axis=0, tiled=True)
    second_move = lax.all_to_all(first_move, "col", split_axis=0, concat_axis=1, tiled=True)
    third_move = lax.all_to_all(second_move, "row", split_axis=1, concat_axis=2, tiled=True)
    other = jnp.einsum("bap,pq->abq", third_move, swapper, preferred_element_type=jnp.float32)
    energy_a = lax.dynamic_slice_in_dim(virt_energy, row_at * tile_a, tile_a, 0)
    energy_b = lax.dynamic_slice_in_dim(virt_energy, col_at * tile_b, tile_b, 0)
    pair_energy = (occ_energy[:, None] + occ_energy[None, :]).reshape(pairs)
    denom = energy_a[:, None, None] + energy_b[None, :, None] - pair_energy[None, None, :]
    return ((ladder.astype(jnp.float32) + other) / denom).astype(jnp.bfloat16)


def chip_at(x, y, z, core):
    return (
        y * 2 + lax.div(x, 2),
        lax.rem(x, 2) * 16 + z * 2 + core,
    )


def mirror_chip(x, y, z):
    return (
        lax.rem(z, 2) * 2 + lax.div(y, 4),
        lax.rem(x, 2) * 4 + lax.div(z, 2),
        lax.rem(y, 4) * 2 + lax.div(x, 2),
    )


def exchange_kernel(
    virt_ref, energy_ref, occ_ref, pair_ref, amp_ref, g_ref,
    t_out, c_out, r_out, ea_out, pe_out, info_ref, eb_ref,
    gbuf, mbuf, stbuf, cf, cbuf, sendf, sbuf, mid, rbuf, blocks, tbuf, tile, tfull, eabuf, pebuf,
    load_sem, out_sem, keep_sem,
    s0_send, s0_recv, s1_send, s1_recv, ring_send, ring_recv, sib_send, sib_recv,
    m1_send, m1_recv, m2_send, m2_recv,
):
    row = lax.axis_index("row")
    col = lax.axis_index("col")
    y, xh = lax.div(row, 2), lax.rem(row, 2)
    xl, core = lax.div(col, 16), lax.rem(col, 2)
    z = lax.div(lax.rem(col, 16), 2)
    x = xh * 2 + xl
    zq, z0 = lax.div(z, 2), lax.rem(z, 2)
    straight = core == xl

    load = pltpu.make_async_copy(g_ref, gbuf, load_sem)
    load.start()

    def remote(src, dst, send, recv, where):
        return pltpu.make_async_remote_copy(
            src_ref=src, dst_ref=dst, send_sem=send, recv_sem=recv,
            device_id=where, device_id_type=MESH,
        )

    def near(d):
        return chip_at(
            lax.rem(x + 2 * (d // 4), 4), y,
            zq * 2 + lax.rem(z0 + (d // 2) % 2, 2), lax.rem(core + d % 2, 2),
        )

    s1_x = jnp.where(straight, x, xh * 2 + 1 - xl)

    def plane(d):
        return chip_at(s1_x, y, lax.rem(z + 2 * d, 8), xl)

    up = chip_at(x, lax.rem(y + 1, 8), z, core)
    down = chip_at(x, lax.rem(y + 7, 8), z, core)
    sibling = chip_at(x, y, z, 1 - core)
    mx, my, mz = mirror_chip(x, y, z)

    def ahead(t):
        dx, dz = DETOURS[t]
        return lax.rem(x + dx, 4), y, lax.rem(z + dz, 8)

    def behind(t):
        dx, dz = DETOURS[t]
        return lax.rem(x + 4 - dx, 4), y, lax.rem(z + 8 - dz, 8)

    def is_here(chip, k):
        return (chip[0] == x) & (chip[1] == y) & (chip[2] == z) & (k == core)

    targets = [mirror_chip(*behind(t)) for t in range(PIECES)]
    feeders = [
        (lax.rem(mx + DETOURS[t][0], 4), my, lax.rem(mz + DETOURS[t][1], 8))
        for t in range(PIECES)
    ]

    barrier = pltpu.get_barrier_semaphore()

    def greet(where):
        pl.semaphore_signal(barrier, inc=1, device_id=where, device_id_type=MESH)

    for t in range(PIECES):
        for k in range(2):
            @pl.when(jnp.logical_not(is_here(feeders[t], k)))
            def _():
                greet(chip_at(*feeders[t], k))
    for t in range(1, PIECES):
        greet(chip_at(*behind(t), core))
    for d in range(1, 4):
        greet(plane(d))

    @pl.when(jnp.logical_not(straight))
    def _():
        greet(plane(0))

    greet(up)
    greet(down)
    for d in range(1, 8):
        greet(near(d))

    a_at, b_at = row * 50, col * 25
    la0, la1 = virt_ref[a_at], virt_ref[a_at + 49]
    lb0, lb1 = virt_ref[b_at], virt_ref[b_at + 24]
    sa = lax.fori_loop(0, 50, lambda i, n: n + jnp.where(virt_ref[a_at + i] == la0, 1, 0), jnp.int32(0))
    sb = lax.fori_loop(0, 25, lambda i, n: n + jnp.where(virt_ref[b_at + i] == lb0, 1, 0), jnp.int32(0))

    pair = pair_ref[...]
    slab = pair.shape[1]
    starts = [jnp.int32(0)]
    for g in range(1, 8):
        starts.append(jnp.sum(jnp.where(pair < g, 1.0, 0.0)).astype(I32))
    ends = starts[1:] + [jnp.int32(slab)]
    bases = [jnp.minimum(lax.div(s, 16) * 16, slab - WIDE) for s in starts]
    base_of = jnp.zeros_like(pair)
    fits = jnp.int32(1)
    for g in range(8):
        base_of = jnp.where(pair >= g, bases[g], base_of)
        fits = jnp.where(ends[g] - bases[g] > WIDE, 0, fits)
    slot_of = lax.broadcasted_iota(I32, pair.shape, 1) - base_of
    stbuf[...] = jnp.where(
        lax.broadcasted_iota(I32, (WIDE, slab), 0) == slot_of, 1.0, 0.0
    ).astype(BF)

    info_ref[0] = fits
    info_ref[1] = sa
    info_ref[2] = sb
    for ja, la in enumerate((la0, la1)):
        for jb, lb in enumerate((lb0, lb1)):
            label = la ^ lb
            base = jnp.int32(0)
            for g in range(1, 8):
                base = jnp.where(label == g, bases[g], base)
            info_ref[4 + 2 * ja + jb] = base

    amp = amp_ref[...].astype(F32)
    packed = jnp.concatenate([amp[0:10], amp[10:20]], axis=1)
    packed = jnp.concatenate([packed, jnp.zeros((6, 128), F32)], axis=0).astype(BF)
    mine = xh * 4 + z0 * 2 + core
    blocks[mine] = packed

    mbuf[...] = jnp.zeros_like(mbuf)
    load.wait()
    first_part = lax.broadcasted_iota(I32, (50, slab), 0) < sa

    def squeeze(i, carry):
        for bb in range(5):
            b = i * 5 + bb
            lb = jnp.where(b < sb, lb0, lb1)
            label = jnp.where(first_part, la0 ^ lb, la1 ^ lb)
            tile = gbuf[b].astype(F32)
            mbuf[bb, 0:50, :] = jnp.where(label == pair, tile, 0.0).astype(BF)
        short = lax.dot_general(
            mbuf[...].reshape(320, slab), stbuf[...], (((1,), (1,)), ((), ())),
            preferred_element_type=F32,
        )
        at = pl.multiple_of(i * 320, 320)
        cf[pl.ds(at, 320), :] = short
        cbuf[pl.ds(at, 320), :] = short.astype(BF)
        return carry

    lax.fori_loop(0, 5, squeeze, 0)
    for h in range(2):
        sendf[h, 624:640, :] = jnp.zeros((16, 128), F32)
        for i in range(25):
            sendf[h, 25 * i:25 * i + 25, :] = cf[pl.ds(25 * h + i, 25, stride=64), :]
        sbuf[h] = sendf[h].astype(BF).reshape(PIECES, PIECE, WIDE)

    expected = jnp.where(straight, PIECES - 1 + 3 + 2 + 7, PIECES + 3 + 2 + 7)
    for t in range(PIECES):
        for k in range(2):
            expected = expected + jnp.where(is_here(targets[t], k), 0, 1)
    pl.semaphore_wait(barrier, expected)

    near_copies = [
        remote(blocks.at[mine], blocks.at[mine], s0_send.at[d - 1], s0_recv.at[mine], near(d))
        for d in range(1, 8)
    ]
    for copy in near_copies:
        copy.start()

    def leg1(h, t):
        return remote(
            sbuf.at[h, t], mid.at[h, t], m1_send.at[h, t], m1_recv.at[h, t],
            chip_at(*ahead(t), core),
        )

    def leg2(h, t, slot):
        source = sbuf if t == 0 else mid
        return remote(
            source.at[h, t], rbuf.at[slot, t], m2_send.at[h, t], m2_recv.at[slot, t],
            chip_at(*targets[t], h),
        )

    def keep_copy(h, t, slot):
        source = sbuf if t == 0 else mid
        return pltpu.make_async_copy(source.at[h, t], rbuf.at[slot, t], keep_sem.at[h, t])

    def forward(h, t):
        if t > 0:
            leg1(h, t).wait_recv()
        here = is_here(targets[t], h)

        @pl.when(jnp.logical_not(here))
        def _():
            leg2(h, t, core).start()

        @pl.when(here)
        def _():
            keep_copy(h, t, core).start()

    for t in range(1, PIECES):
        for h in range(2):
            leg1(h, t).start()
    for h in range(2):
        forward(h, 0)

    def near_arrived(s):
        @pl.when(s != mine)
        def _():
            remote(blocks.at[s], blocks.at[s], s0_send.at[0], s0_recv.at[s], sibling).wait_recv()

    for s in range(8):
        near_arrived(s)
    left = lax.broadcasted_iota(I32, (10, 128), 1) < 64
    for q in range(4):
        lo = blocks[q].astype(F32)[0:10]
        hi = blocks[4 + q].astype(F32)[0:10]
        tbuf[20 * q:20 * q + 10, :] = jnp.where(left, lo, pltpu.roll(hi, 64, 1))
        tbuf[20 * q + 10:20 * q + 20, :] = jnp.where(left, pltpu.roll(lo, 64, 1), hi)

    def part(half, quarter, yy):
        at = pl.multiple_of(half * 320 + quarter * 80, 80)
        return tfull.at[pl.ds(at, 80), pl.ds(pl.multiple_of(yy * 128, 128), 128)]

    own_at = pl.multiple_of(xl * 320 + zq * 80, 80)
    lane_at = pl.multiple_of(y * 128, 128)
    tile[...] = tbuf[...].astype(BF)

    @pl.when(straight)
    def _():
        tfull[pl.ds(own_at, 80), pl.ds(lane_at, 128)] = tile[...]

    def spread(d):
        return remote(
            tile, part(xl, zq, y), s1_send.at[d], s1_recv.at[d], plane(d)
        )

    @pl.when(jnp.logical_not(straight))
    def _():
        spread(0).start()

    for d in (1, 3, 2):
        spread(d).start()

    def ring(d, away, sign):
        block = part(core, lax.rem(zq + 4 - d, 4), lax.rem(y + 8 - away * sign, 8))
        index = away if sign > 0 else 8 - away
        return index, block

    def ring_copy(d, step, sign):
        _, block = ring(d, step - 1, sign)
        slot = 2 * step + (sign > 0) - 2
        return remote(
            block, block, ring_send.at[d, slot], ring_recv.at[d, slot],
            up if sign > 0 else down,
        )

    def last_step(d, sign):
        return 4 if (sign > 0) == (d < 2) else 3

    def to_sibling(away, sign):
        yy = lax.rem(y + 8 - away * sign, 8)
        rows = pl.ds(pl.multiple_of(core * 320, 320), 320)
        block = tfull.at[rows, pl.ds(pl.multiple_of(yy * 128, 128), 128)]
        slot = away if sign > 0 else 8 - away
        return remote(block, block, sib_send.at[slot], sib_recv.at[slot], sibling)

    order = (0, 1, 3, 2)
    for d in order:
        if d == 0:
            @pl.when(jnp.logical_not(straight))
            def _():
                spread(0).wait_recv()
        else:
            spread(d).wait_recv()
        for sign in (1, -1):
            ring_copy(d, 1, sign).start()
    to_sibling(0, 1).start()

    def around(step):
        for d in order:
            for sign in (1, -1):
                if step <= last_step(d, sign):
                    ring_copy(d, step, sign).wait_recv()
                    if step + 1 <= last_step(d, sign):
                        ring_copy(d, step + 1, sign).start()
        for sign in (1, -1):
            if step < 4 or sign > 0:
                to_sibling(step, sign).start()

    def deliver(ts):
        for t in ts:
            for h in range(2):
                forward(h, t)

    deliver((1, 2))
    around(1)
    deliver((3, 4))
    around(2)
    deliver((5, 6))
    around(3)
    deliver((7,))
    around(4)

    lane8 = lax.broadcasted_iota(I32, (8, 1024), 1)
    first, second = lax.div(lane8, 32), lax.rem(lane8, 32)
    pe = jnp.zeros((8, 1024), F32)
    for i in range(32):
        pe = pe + jnp.where(first == i, occ_ref[i], 0.0) + jnp.where(second == i, occ_ref[i], 0.0)
    pebuf[...] = pe
    sub = lax.broadcasted_iota(I32, (64, 128), 0)
    ea = jnp.ones((64, 128), F32)
    for i in range(50):
        ea = jnp.where(sub == i, energy_ref[a_at + i], ea)
    eabuf[...] = ea

    def copy_eb(i, carry):
        eb_ref[i] = energy_ref[b_at + i]
        return carry

    lax.fori_loop(0, 25, copy_eb, 0)

    for slot in range(8):
        step = slot if slot <= 4 else 8 - slot
        to_sibling(step, 1 if slot <= 4 else -1).wait_recv()
    outs = [
        pltpu.make_async_copy(tfull, t_out, out_sem.at[0]),
        pltpu.make_async_copy(cbuf, c_out, out_sem.at[1]),
        pltpu.make_async_copy(eabuf, ea_out, out_sem.at[2]),
        pltpu.make_async_copy(pebuf, pe_out, out_sem.at[3]),
    ]
    for copy in outs:
        copy.start()
    for t in range(PIECES):
        here = [is_here(feeders[t], k) for k in range(2)]
        for k in range(2):
            @pl.when(jnp.logical_not(here[k]))
            def _():
                remote(
                    mid.at[0, t], rbuf.at[k, t], m2_send.at[0, t], m2_recv.at[k, t], sibling
                ).wait_recv()
    for t in range(PIECES):
        for h in range(2):
            here = is_here(targets[t], h)

            @pl.when(here)
            def _():
                keep_copy(h, t, core).wait()

            @pl.when(jnp.logical_not(here))
            def _():
                leg2(h, t, core).wait_send()
            if t > 0:
                leg1(h, t).wait_send()
    last = pltpu.make_async_copy(rbuf, r_out, out_sem.at[4])
    last.start()
    for copy in near_copies:
        copy.wait_send()

    @pl.when(jnp.logical_not(straight))
    def _():
        spread(0).wait_send()

    for d in (1, 3, 2):
        spread(d).wait_send()
    for d in range(4):
        for sign in (1, -1):
            for step in range(1, last_step(d, sign) + 1):
                ring_copy(d, step, sign).wait_send()
    for slot in range(8):
        step = slot if slot <= 4 else 8 - slot
        to_sibling(step, 1 if slot <= 4 else -1).wait_send()
    for copy in outs:
        copy.wait()
    last.wait()


def exchange(g, amp, virt_irrep, pair_irrep, virt_energy, occ_energy):
    dma, vmem = pltpu.SemaphoreType.DMA, pltpu.VMEM
    smem_spec = pl.BlockSpec(memory_space=pltpu.SMEM)
    vmem_spec = pl.BlockSpec(memory_space=pltpu.VMEM)
    any_spec = pl.BlockSpec(memory_space=pl.ANY)
    return pl.pallas_call(
        exchange_kernel,
        name="exchange",
        out_shape=[
            jax.ShapeDtypeStruct((640, 1024), BF),
            jax.ShapeDtypeStruct((1600, WIDE), BF),
            jax.ShapeDtypeStruct((2, PIECES, PIECE, WIDE), BF),
            jax.ShapeDtypeStruct((64, 128), F32),
            jax.ShapeDtypeStruct((8, 1024), F32),
            jax.ShapeDtypeStruct((8,), I32),
            jax.ShapeDtypeStruct((32,), F32),
        ],
        in_specs=[smem_spec, smem_spec, smem_spec, vmem_spec, vmem_spec, any_spec],
        out_specs=[any_spec] * 5 + [smem_spec] * 2,
        scratch_shapes=[
            vmem((25, 50, 640), BF),
            vmem((5, 64, 640), BF),
            vmem((WIDE, 640), BF),
            vmem((1600, WIDE), F32),
            vmem((1600, WIDE), BF),
            vmem((2, 640, WIDE), F32),
            vmem((2, PIECES, PIECE, WIDE), BF),
            vmem((2, PIECES, PIECE, WIDE), BF),
            vmem((2, PIECES, PIECE, WIDE), BF),
            vmem((8, 16, 128), BF),
            vmem((80, 128), F32),
            vmem((80, 128), BF),
            vmem((640, 1024), BF),
            vmem((64, 128), F32),
            vmem((8, 1024), F32),
            dma, dma((5,)), dma((2, PIECES)),
            dma((7,)), dma((8,)), dma((4,)), dma((4,)), dma((4, 8)), dma((4, 8)),
            dma((8,)), dma((8,)),
            dma((2, PIECES)), dma((2, PIECES)), dma((2, PIECES)), dma((2, PIECES)),
        ],
        compiler_params=pltpu.CompilerParams(
            collective_id=1, has_side_effects=True, vmem_limit_bytes=48 << 20
        ),
    )(virt_irrep, virt_energy, occ_energy, pair_irrep.reshape(1, -1), amp, g)


def ladder_kernel(info, eb, c_ref, r_ref, t_ref, swap_ref, ea_ref, pe_ref, out_ref, xmf, xall, rhs, acc):
    step = pl.program_id(0)
    sa, sb = info[1], info[2]
    two_a = sa < 50
    two_b = sb < 25

    @pl.when(step == 0)
    def _():
        xmf[...] = jnp.zeros_like(xmf)
        for k in range(2):
            block = r_ref[k].astype(F32)
            for b in range(25):
                xmf[64 * b + 25 * k:64 * b + 25 * k + 25, :] = block[25 * b:25 * b + 25]
        xall[:, 0:WIDE] = c_ref[...]
        xall[:, WIDE:2 * WIDE] = xmf[...].astype(BF)
        for ja in range(2):
            for jb in range(2):
                def fill(ja=ja, jb=jb):
                    base = pl.multiple_of(info[4 + 2 * ja + jb], 16)
                    own = t_ref[pl.ds(base, WIDE), :]
                    rhs[2 * ja + jb, 0:WIDE, :] = own
                    rhs[2 * ja + jb, WIDE:2 * WIDE, :] = jnp.dot(
                        own, swap_ref[...], preferred_element_type=F32
                    ).astype(BF)

                needed = True if ja + jb == 0 else (two_a if jb == 0 else two_b if ja == 0 else two_a & two_b)
                if needed is True:
                    fill()
                else:
                    pl.when(needed)(fill)

    b0 = step * 5
    at = pl.multiple_of(step * 320, 320)
    place = lax.broadcasted_iota(I32, (320, 2 * WIDE), 0)
    in_a = lax.rem(place, 64) >= sa
    in_b = b0 + lax.div(place, 64) >= sb

    def product(ja, jb):
        side_a = in_a if ja else jnp.logical_not(in_a)
        side_b = jnp.where(in_b, 1, 0) == jb
        lhs = jnp.where(side_a & side_b, xall[pl.ds(at, 320), :].astype(F32), 0.0).astype(BF)
        return jnp.dot(lhs, rhs[2 * ja + jb], preferred_element_type=F32)

    lead = jnp.where(b0 >= sb, 1, 0)
    straddle = (b0 < sb) & (b0 + 5 > sb)
    acc[...] = product(0, lead)

    @pl.when(two_a)
    def _():
        acc[...] += product(1, lead)

    @pl.when(straddle)
    def _():
        acc[...] += product(0, 1)

    @pl.when(straddle & two_a)
    def _():
        acc[...] += product(1, 1)

    pe = pe_ref[0:1, :]
    for bb in range(5):
        ea = ea_ref[0:50, 0:1] + eb[b0 + bb]
        out_ref[bb] = (acc[64 * bb:64 * bb + 50, :] / (ea - pe)).astype(BF)


def ladder(t, c, r, ea, pe, info, eb, swap):
    whole = lambda shape: pl.BlockSpec(shape, lambda i, *_: (0,) * len(shape))
    return pl.pallas_call(
        ladder_kernel,
        name="ladder",
        grid_spec=pltpu.PrefetchScalarGridSpec(
            num_scalar_prefetch=2,
            grid=(5,),
            in_specs=[
                whole((1600, WIDE)), whole((2, 640, WIDE)), whole((640, 1024)),
                whole((1024, 1024)), whole((64, 128)), whole((8, 1024)),
            ],
            out_specs=pl.BlockSpec((5, 50, 1024), lambda i, *_: (i, 0, 0)),
            scratch_shapes=[
                pltpu.VMEM((1600, WIDE), F32),
                pltpu.VMEM((1600, 2 * WIDE), BF),
                pltpu.VMEM((4, 2 * WIDE, 1024), BF),
                pltpu.VMEM((320, 1024), F32),
            ],
        ),
        out_shape=jax.ShapeDtypeStruct((25, 50, 1024), BF),
        compiler_params=pltpu.CompilerParams(vmem_limit_bytes=48 << 20),
    )(info, eb, c, r.reshape(2, 640, WIDE), t, swap, ea, pe)


def per_device(integrals, amplitudes, virt_irrep, pair_irrep, virt_energy, occ_energy):
    g = jnp.transpose(integrals, (1, 0, 2))
    t, c, r, ea, pe, info, eb = exchange(
        g, amplitudes.T, virt_irrep, pair_irrep, virt_energy, occ_energy
    )
    source = np.arange(1024)
    target = source % 32 * 32 + source // 32
    swap = jnp.asarray((source[:, None] == target[None, :]).astype(jnp.bfloat16))

    def short(_):
        return ladder(t, c, r, ea, pe, info, eb, swap)

    def general(_):
        return jnp.transpose(
            long_runs(integrals, amplitudes, virt_irrep, pair_irrep, virt_energy, occ_energy),
            (1, 0, 2),
        )

    out = lax.cond(info[0] == 1, short, general, 0)
    return jnp.transpose(out, (1, 0, 2))


def solution(mesh):
    return jax.shard_map(
        per_device,
        mesh=mesh,
        in_specs=(P("row", "col", None), P("row", "col"), P(), P(), P(), P()),
        out_specs=P("row", "col", None),
        check_vma=False,
    )
```

```python
import functools

import jax
import jax.numpy as jnp
import numpy as np
from jax import lax
from jax.experimental import pallas as pl
from jax.experimental.pallas import tpu as pltpu
from jax.sharding import PartitionSpec as P

MESH = pl.DeviceIdType.MESH
BF = jnp.bfloat16
F32 = jnp.float32
I32 = jnp.int32
WIDE = 128
RUN = 96
PIECES = 6
PIECE = 80
SPREAD = 8


def pair_swapper(occupied):
    pairs = occupied * occupied
    source = jnp.arange(pairs, dtype=jnp.int32)
    target = source % occupied * occupied + source // occupied
    return (source[:, None] == target[None, :]).astype(jnp.bfloat16)


def long_runs(integrals, amplitudes, virt_irrep, pair_irrep, virt_energy, occ_energy):
    tile_a, tile_b, slab = integrals.shape
    occupied = occ_energy.shape[0]
    pairs = occupied * occupied
    row_at = lax.axis_index("row")
    col_at = lax.axis_index("col")
    labels_a = lax.dynamic_slice_in_dim(virt_irrep, row_at * tile_a, tile_a, 0)
    labels_b = lax.dynamic_slice_in_dim(virt_irrep, col_at * tile_b, tile_b, 0)
    keep = (
        jnp.bitwise_xor(labels_a[:, None, None], labels_b[None, :, None])
        == pair_irrep[None, None, :]
    )
    masked = jnp.where(keep, integrals, jnp.zeros((), integrals.dtype))
    flat = masked.reshape(tile_a * tile_b, slab)
    swapper = pair_swapper(occupied)
    all_pairs = lax.all_gather(amplitudes, "row", axis=0, tiled=True)
    totals = lax.dot_general(
        flat,
        lax.all_gather(all_pairs, "col", axis=1, tiled=True),
        (((1,), (1,)), ((), ())),
        preferred_element_type=jnp.float32,
    )
    rounded = totals.astype(jnp.bfloat16)
    ladder = rounded.reshape(tile_a, tile_b, pairs)
    first_move = lax.all_to_all(ladder, "row", split_axis=2, concat_axis=0, tiled=True)
    second_move = lax.all_to_all(first_move, "col", split_axis=0, concat_axis=1, tiled=True)
    third_move = lax.all_to_all(second_move, "row", split_axis=1, concat_axis=2, tiled=True)
    other = jnp.einsum("bap,pq->abq", third_move, swapper, preferred_element_type=jnp.float32)
    energy_a = lax.dynamic_slice_in_dim(virt_energy, row_at * tile_a, tile_a, 0)
    energy_b = lax.dynamic_slice_in_dim(virt_energy, col_at * tile_b, tile_b, 0)
    pair_energy = (occ_energy[:, None] + occ_energy[None, :]).reshape(pairs)
    denom = energy_a[:, None, None] + energy_b[None, :, None] - pair_energy[None, None, :]
    return ((ladder.astype(jnp.float32) + other) / denom).astype(jnp.bfloat16)


def chip_at(x, y, z, core):
    return (
        y * 2 + lax.div(x, 2),
        lax.rem(x, 2) * 16 + z * 2 + core,
    )


def mirror_chip(x, y, z):
    return (
        lax.rem(z, 2) * 2 + lax.div(y, 4),
        lax.rem(x, 2) * 4 + lax.div(z, 2),
        lax.rem(y, 4) * 2 + lax.div(x, 2),
    )


def exchange_kernel(
    virt_ref, energy_ref, occ_ref, pair_ref, amp_ref, g_ref, swap_ref,
    t_out, ts_out, c_out, r_out, ea_out, pe_out, info_ref, eb_ref,
    gbuf, mbuf, stbuf, swapbuf, cf, cbuf, sendf, sbuf, mid, rbuf, blocks, tbuf, tile, tfull, tswap, eabuf, pebuf,
    load_sem, swap_sem, out_sem, keep_sem,
    s0_send, s0_recv, s1_send, s1_recv, ring_send, ring_recv, sib_send, sib_recv,
    m1_send, m1_recv, m2_send, m2_recv,
):
    row = lax.axis_index("row")
    col = lax.axis_index("col")
    y, xh = lax.div(row, 2), lax.rem(row, 2)
    xl, core = lax.div(col, 16), lax.rem(col, 2)
    z = lax.div(lax.rem(col, 16), 2)
    x = xh * 2 + xl
    zq, z0 = lax.div(z, 2), lax.rem(z, 2)
    straight = core == xl

    load = pltpu.make_async_copy(g_ref, gbuf, load_sem)
    load.start()
    load_swap = pltpu.make_async_copy(swap_ref, swapbuf, swap_sem)
    load_swap.start()

    def remote(src, dst, send, recv, where):
        return pltpu.make_async_remote_copy(
            src_ref=src, dst_ref=dst, send_sem=send, recv_sem=recv,
            device_id=where, device_id_type=MESH,
        )

    def near(d):
        return chip_at(
            lax.rem(x + 2 * (d // 4), 4), y,
            zq * 2 + lax.rem(z0 + (d // 2) % 2, 2), lax.rem(core + d % 2, 2),
        )

    s1_x = jnp.where(straight, x, xh * 2 + 1 - xl)

    def plane(d):
        return chip_at(s1_x, y, lax.rem(z + 2 * d, 8), xl)

    up = chip_at(x, lax.rem(y + 1, 8), z, core)
    down = chip_at(x, lax.rem(y + 7, 8), z, core)
    sibling = chip_at(x, y, z, 1 - core)
    mx, my, mz = mirror_chip(x, y, z)

    def detour(k, h, t):
        return lax.rem(4 * k + PIECES * h + t, SPREAD)

    def ahead(d):
        return lax.rem(x + d + 1, 4), y, lax.rem(z + d, 8)

    def behind(d):
        return lax.rem(x + 11 - d, 4), y, lax.rem(z + 8 - d, 8)

    def beside_mirror(d):
        return lax.rem(mx + d + 1, 4), my, lax.rem(mz + d, 8)

    def is_here(chip, k):
        return (chip[0] == x) & (chip[1] == y) & (chip[2] == z) & (k == core)

    slots = [(h, t) for t in range(PIECES) for h in range(2)]
    targets = {(h, t): mirror_chip(*behind(detour(core, h, t))) for h, t in slots}
    feeders = {(k, t): beside_mirror(detour(k, core, t)) for k, t in slots}

    barrier = pltpu.get_barrier_semaphore()

    def greet(where):
        pl.semaphore_signal(barrier, inc=1, device_id=where, device_id_type=MESH)

    for k, t in slots:
        @pl.when(jnp.logical_not(is_here(feeders[k, t], k)))
        def _():
            greet(chip_at(*feeders[k, t], k))
    for d in range(SPREAD):
        greet(chip_at(*behind(d), core))
    for d in range(1, 4):
        greet(plane(d))

    @pl.when(jnp.logical_not(straight))
    def _():
        greet(plane(0))

    greet(up)
    greet(down)
    for d in range(1, 8):
        greet(near(d))

    a_at, b_at = row * 50, col * 25
    la0, la1 = virt_ref[a_at], virt_ref[a_at + 49]
    lb0, lb1 = virt_ref[b_at], virt_ref[b_at + 24]
    sa = lax.fori_loop(0, 50, lambda i, n: n + jnp.where(virt_ref[a_at + i] == la0, 1, 0), jnp.int32(0))
    sb = lax.fori_loop(0, 25, lambda i, n: n + jnp.where(virt_ref[b_at + i] == lb0, 1, 0), jnp.int32(0))

    slab = pair_ref.shape[0]
    pair = pair_ref[...].reshape(1, slab)
    starts = [jnp.int32(0)]
    for g in range(1, 8):
        starts.append(jnp.sum(jnp.where(pair < g, 1.0, 0.0)).astype(I32))
    ends = starts[1:] + [jnp.int32(slab)]
    base_of = jnp.zeros_like(pair)
    fits = jnp.int32(1)
    for g in range(8):
        base_of = jnp.where(pair >= g, starts[g], base_of)
        fits = jnp.where(ends[g] - starts[g] > RUN, 0, fits)
    slot_of = lax.broadcasted_iota(I32, pair.shape, 1) - base_of
    stbuf[...] = jnp.where(
        lax.broadcasted_iota(I32, (WIDE, slab), 0) == slot_of, 1.0, 0.0
    ).astype(BF)

    info_ref[0] = fits
    info_ref[1] = sa
    info_ref[2] = sb
    for ja, la in enumerate((la0, la1)):
        for jb, lb in enumerate((lb0, lb1)):
            label = la ^ lb
            start = jnp.int32(0)
            for g in range(1, 8):
                start = jnp.where(label == g, starts[g], start)
            info_ref[4 + 2 * ja + jb] = start

    amp = amp_ref[...].astype(F32)
    packed = jnp.concatenate([amp[0:10], amp[10:20]], axis=1)
    packed = jnp.concatenate([packed, jnp.zeros((6, 128), F32)], axis=0).astype(BF)
    mine = xh * 4 + z0 * 2 + core
    blocks[mine] = packed

    mbuf[...] = jnp.zeros_like(mbuf)
    load.wait()
    first_part = lax.broadcasted_iota(I32, (50, slab), 0) < sa

    def squeeze(i, carry):
        for bb in range(5):
            b = i * 5 + bb
            lb = jnp.where(b < sb, lb0, lb1)
            label = jnp.where(first_part, la0 ^ lb, la1 ^ lb)
            tile = gbuf[b].astype(F32)
            mbuf[bb, 0:50, :] = jnp.where(label == pair, tile, 0.0).astype(BF)
        short = lax.dot_general(
            mbuf[...].reshape(320, slab), stbuf[...], (((1,), (1,)), ((), ())),
            preferred_element_type=F32,
        )
        at = pl.multiple_of(i * 320, 320)
        cf[pl.ds(at, 320), :] = short
        cbuf[pl.ds(at, 320), :] = short.astype(BF)
        return carry

    lax.fori_loop(0, 5, squeeze, 0)
    for h in range(2):
        sendf[h, 624:640, :] = jnp.zeros((16, 128), F32)
        for i in range(25):
            sendf[h, 25 * i:25 * i + 25, :] = cf[pl.ds(25 * h + i, 25, stride=64), :]
        quarter = [sendf[h, 160 * i:160 * i + 160, :] for i in range(4)]
        turned = [pltpu.roll(quarter[i], WIDE - 32 * i, 1) for i in range(1, 4)]
        lane = lax.broadcasted_iota(I32, (160, WIDE), 1)
        sheets = [
            jnp.where(lane < 96, quarter[0], turned[0]),
            jnp.where(lane < 64, turned[0], turned[1]),
            jnp.where(lane < 32, turned[1], turned[2]),
        ]
        for i in range(3):
            sbuf[h, 2 * i:2 * i + 2] = sheets[i].astype(BF).reshape(2, PIECE, WIDE)

    expected = jnp.where(straight, SPREAD + 3 + 2 + 7, SPREAD + 4 + 2 + 7)
    for h, t in slots:
        expected = expected + jnp.where(is_here(targets[h, t], h), 0, 1)
    pl.semaphore_wait(barrier, expected)

    near_copies = [
        remote(blocks.at[mine], blocks.at[mine], s0_send.at[d - 1], s0_recv.at[mine], near(d))
        for d in range(1, 8)
    ]
    for copy in near_copies:
        copy.start()

    def leg1(h, t):
        return remote(
            sbuf.at[h, t], mid.at[h, t], m1_send.at[h, t], m1_recv.at[h, t],
            chip_at(*ahead(detour(core, h, t)), core),
        )

    def leg2(h, t):
        return remote(
            mid.at[h, t], rbuf.at[core, t], m2_send.at[h, t], m2_recv.at[core, t],
            chip_at(*targets[h, t], h),
        )

    def keep_copy(h, t):
        return pltpu.make_async_copy(mid.at[h, t], rbuf.at[core, t], keep_sem.at[h, t])

    def forward(h, t):
        leg1(h, t).wait_recv()
        here = is_here(targets[h, t], h)

        @pl.when(jnp.logical_not(here))
        def _():
            leg2(h, t).start()

        @pl.when(here)
        def _():
            keep_copy(h, t).start()

    def near_arrived(s):
        @pl.when(s != mine)
        def _():
            remote(blocks.at[s], blocks.at[s], s0_send.at[0], s0_recv.at[s], sibling).wait_recv()

    for s in range(8):
        near_arrived(s)
    left = lax.broadcasted_iota(I32, (10, 128), 1) < 64
    for q in range(4):
        lo = blocks[q].astype(F32)[0:10]
        hi = blocks[4 + q].astype(F32)[0:10]
        tbuf[20 * q:20 * q + 10, :] = jnp.where(left, lo, pltpu.roll(hi, 64, 1))
        tbuf[20 * q + 10:20 * q + 20, :] = jnp.where(left, pltpu.roll(lo, 64, 1), hi)

    def part(half, quarter, yy):
        at = pl.multiple_of(half * 320 + quarter * 80, 80)
        return tfull.at[pl.ds(at, 80), pl.ds(pl.multiple_of(yy * 128, 128), 128)]

    own_at = pl.multiple_of(xl * 320 + zq * 80, 80)
    lane_at = pl.multiple_of(y * 128, 128)
    tile[...] = tbuf[...].astype(BF)

    @pl.when(straight)
    def _():
        tfull[pl.ds(own_at, 80), pl.ds(lane_at, 128)] = tile[...]

    def spread(d):
        return remote(
            tile, part(xl, zq, y), s1_send.at[d], s1_recv.at[d], plane(d)
        )

    @pl.when(jnp.logical_not(straight))
    def _():
        spread(0).start()

    for d in (1, 3, 2):
        spread(d).start()

    def ring(d, away, sign):
        block = part(core, lax.rem(zq + 4 - d, 4), lax.rem(y + 8 - away * sign, 8))
        index = away if sign > 0 else 8 - away
        return index, block

    def ring_copy(d, step, sign):
        _, block = ring(d, step - 1, sign)
        slot = 2 * step + (sign > 0) - 2
        return remote(
            block, block, ring_send.at[d, slot], ring_recv.at[d, slot],
            up if sign > 0 else down,
        )

    def last_step(d, sign):
        return 4 if (sign > 0) == (d < 2) else 3

    def to_sibling(away, sign):
        yy = lax.rem(y + 8 - away * sign, 8)
        rows = pl.ds(pl.multiple_of(core * 320, 320), 320)
        block = tfull.at[rows, pl.ds(pl.multiple_of(yy * 128, 128), 128)]
        slot = away if sign > 0 else 8 - away
        return remote(block, block, sib_send.at[slot], sib_recv.at[slot], sibling)

    order = (0, 1, 3, 2)
    for d in order:
        if d == 0:
            @pl.when(jnp.logical_not(straight))
            def _():
                spread(0).wait_recv()
        else:
            spread(d).wait_recv()
        for sign in (1, -1):
            ring_copy(d, 1, sign).start()
    to_sibling(0, 1).start()

    def around(step):
        for d in order:
            for sign in (1, -1):
                if step <= last_step(d, sign):
                    ring_copy(d, step, sign).wait_recv()
                    if step + 1 <= last_step(d, sign):
                        ring_copy(d, step + 1, sign).start()
        for sign in (1, -1):
            if step < 4 or sign > 0:
                to_sibling(step, sign).start()

    def deliver(ts):
        for t in ts:
            for h in range(2):
                forward(h, t)

    for h, t in slots:
        leg1(h, t).start()

    around(1)
    around(2)
    deliver((0, 1, 2))
    around(3)
    deliver((3, 4, 5))
    around(4)

    lane8 = lax.broadcasted_iota(I32, (8, 1024), 1)
    first, second = lax.div(lane8, 32), lax.rem(lane8, 32)
    pe = jnp.zeros((8, 1024), F32)
    for i in range(32):
        pe = pe + jnp.where(first == i, occ_ref[i], 0.0) + jnp.where(second == i, occ_ref[i], 0.0)
    pebuf[...] = pe
    sub = lax.broadcasted_iota(I32, (64, 128), 0)
    ea = jnp.ones((64, 128), F32)
    for i in range(50):
        ea = jnp.where(sub == i, energy_ref[a_at + i], ea)
    eabuf[...] = ea

    def copy_eb(i, carry):
        eb_ref[i] = energy_ref[b_at + i]
        return carry

    lax.fori_loop(0, 25, copy_eb, 0)

    for slot in range(8):
        step = slot if slot <= 4 else 8 - slot
        to_sibling(step, 1 if slot <= 4 else -1).wait_recv()
    load_swap.wait()

    def swapped(i, carry):
        at = pl.multiple_of(i * 128, 128)
        tswap[pl.ds(at, 128), :] = jnp.dot(
            tfull[pl.ds(at, 128), :], swapbuf[...], preferred_element_type=F32
        ).astype(BF)
        return carry

    lax.fori_loop(0, 5, swapped, 0)
    outs = [
        pltpu.make_async_copy(tfull, t_out, out_sem.at[0]),
        pltpu.make_async_copy(tswap, ts_out, out_sem.at[5]),
        pltpu.make_async_copy(cbuf, c_out, out_sem.at[1]),
        pltpu.make_async_copy(eabuf, ea_out, out_sem.at[2]),
        pltpu.make_async_copy(pebuf, pe_out, out_sem.at[3]),
    ]
    for copy in outs:
        copy.start()
    for k, t in slots:
        @pl.when(jnp.logical_not(is_here(feeders[k, t], k)))
        def _():
            remote(
                mid.at[0, t], rbuf.at[k, t], m2_send.at[0, t], m2_recv.at[k, t], sibling
            ).wait_recv()
    for h, t in slots:
        here = is_here(targets[h, t], h)

        @pl.when(here)
        def _():
            keep_copy(h, t).wait()

        @pl.when(jnp.logical_not(here))
        def _():
            leg2(h, t).wait_send()

        leg1(h, t).wait_send()
    last = pltpu.make_async_copy(rbuf, r_out, out_sem.at[4])
    last.start()
    for copy in near_copies:
        copy.wait_send()

    @pl.when(jnp.logical_not(straight))
    def _():
        spread(0).wait_send()

    for d in (1, 3, 2):
        spread(d).wait_send()
    for d in range(4):
        for sign in (1, -1):
            for step in range(1, last_step(d, sign) + 1):
                ring_copy(d, step, sign).wait_send()
    for slot in range(8):
        step = slot if slot <= 4 else 8 - slot
        to_sibling(step, 1 if slot <= 4 else -1).wait_send()
    for copy in outs:
        copy.wait()
    last.wait()


def exchange(g, amp, virt_irrep, pair_irrep, virt_energy, occ_energy, swap):
    dma, vmem = pltpu.SemaphoreType.DMA, pltpu.VMEM
    smem_spec = pl.BlockSpec(memory_space=pltpu.SMEM)
    vmem_spec = pl.BlockSpec(memory_space=pltpu.VMEM)
    any_spec = pl.BlockSpec(memory_space=pl.ANY)
    return pl.pallas_call(
        exchange_kernel,
        name="exchange",
        out_shape=[
            jax.ShapeDtypeStruct((640, 1024), BF),
            jax.ShapeDtypeStruct((640, 1024), BF),
            jax.ShapeDtypeStruct((1600, WIDE), BF),
            jax.ShapeDtypeStruct((2, PIECES, PIECE, WIDE), BF),
            jax.ShapeDtypeStruct((64, 128), F32),
            jax.ShapeDtypeStruct((8, 1024), F32),
            jax.ShapeDtypeStruct((8,), I32),
            jax.ShapeDtypeStruct((32,), F32),
        ],
        in_specs=[smem_spec, smem_spec, smem_spec, vmem_spec, vmem_spec, any_spec, any_spec],
        out_specs=[any_spec] * 6 + [smem_spec] * 2,
        scratch_shapes=[
            vmem((25, 50, 640), BF),
            vmem((5, 64, 640), BF),
            vmem((WIDE, 640), BF),
            vmem((1024, 1024), BF),
            vmem((1600, WIDE), F32),
            vmem((1600, WIDE), BF),
            vmem((2, 640, WIDE), F32),
            vmem((2, PIECES, PIECE, WIDE), BF),
            vmem((2, PIECES, PIECE, WIDE), BF),
            vmem((2, PIECES, PIECE, WIDE), BF),
            vmem((8, 16, 128), BF),
            vmem((80, 128), F32),
            vmem((80, 128), BF),
            vmem((640, 1024), BF),
            vmem((640, 1024), BF),
            vmem((64, 128), F32),
            vmem((8, 1024), F32),
            dma, dma, dma((6,)), dma((2, PIECES)),
            dma((7,)), dma((8,)), dma((4,)), dma((4,)), dma((4, 8)), dma((4, 8)),
            dma((8,)), dma((8,)),
            dma((2, PIECES)), dma((2, PIECES)), dma((2, PIECES)), dma((2, PIECES)),
        ],
        compiler_params=pltpu.CompilerParams(
            collective_id=1, has_side_effects=True, vmem_limit_bytes=60 << 20
        ),
    )(virt_irrep, virt_energy, occ_energy, pair_irrep, amp, g, swap)


def ladder_kernel(info, eb, c_ref, r_ref, t_ref, ts_ref, ea_ref, pe_ref, out_ref, messf, xall, rhs, acc):
    step = pl.program_id(0)
    sa, sb = info[1], info[2]
    two_a = sa < 50
    two_b = sb < 25

    def base_of(ja, jb):
        start = info[4 + 2 * ja + jb]
        return pl.multiple_of(jnp.minimum(lax.div(start, 16) * 16, t_ref.shape[0] - WIDE), 16)

    @pl.when(step == 0)
    def _():
        lane = lax.broadcasted_iota(I32, (160, WIDE), 1)
        xall[:, 0:WIDE] = c_ref[...].astype(F32)
        xall[:, WIDE:2 * WIDE] = jnp.zeros((1600, WIDE), F32)
        for k in range(2):
            sheets = [r_ref[k, 160 * i:160 * i + 160, :].astype(F32) for i in range(3)]
            messf[0:160, :] = jnp.where(lane < 96, sheets[0], 0.0)
            for i in range(1, 4):
                low = sheets[i] if i < 3 else jnp.zeros((160, WIDE), F32)
                both = jnp.where(
                    lane >= WIDE - 32 * i, sheets[i - 1], jnp.where(lane < 96 - 32 * i, low, 0.0)
                )
                messf[160 * i:160 * i + 160, :] = pltpu.roll(both, 32 * i, 1)
            for b in range(25):
                xall[64 * b + 25 * k:64 * b + 25 * k + 25, WIDE:2 * WIDE] = messf[25 * b:25 * b + 25, :]
        for ja in range(2):
            for jb in range(2):
                def fill(ja=ja, jb=jb):
                    rows = pl.ds(base_of(ja, jb), WIDE)
                    rhs[2 * ja + jb, 0:WIDE, :] = t_ref[rows, :]
                    rhs[2 * ja + jb, WIDE:2 * WIDE, :] = ts_ref[rows, :]

                needed = True if ja + jb == 0 else (two_a if jb == 0 else two_b if ja == 0 else two_a & two_b)
                if needed is True:
                    fill()
                else:
                    pl.when(needed)(fill)

    b0 = step * 5
    at = pl.multiple_of(step * 320, 320)
    place = lax.broadcasted_iota(I32, (320, WIDE), 0)
    in_a = lax.rem(place, 64) >= sa
    in_b = b0 + lax.div(place, 64) >= sb

    def product(ja, jb):
        side_a = in_a if ja else jnp.logical_not(in_a)
        side = side_a & (jnp.where(in_b, 1, 0) == jb)
        turn = info[4 + 2 * ja + jb] - base_of(ja, jb)
        lhs = jnp.concatenate([
            jnp.where(side, pltpu.roll(xall[pl.ds(at, 320), WIDE * i:WIDE * i + WIDE], turn, 1), 0.0).astype(BF)
            for i in range(2)
        ], axis=1)
        return jnp.dot(lhs, rhs[2 * ja + jb], preferred_element_type=F32)

    lead = jnp.where(b0 >= sb, 1, 0)
    straddle = (b0 < sb) & (b0 + 5 > sb)
    acc[...] = product(0, lead)

    @pl.when(two_a)
    def _():
        acc[...] += product(1, lead)

    @pl.when(straddle)
    def _():
        acc[...] += product(0, 1)

    @pl.when(straddle & two_a)
    def _():
        acc[...] += product(1, 1)

    pe = pe_ref[0:1, :]
    for bb in range(5):
        ea = ea_ref[0:50, 0:1] + eb[b0 + bb]
        out_ref[bb] = (acc[64 * bb:64 * bb + 50, :] / (ea - pe)).astype(BF)


def ladder(t, ts, c, r, ea, pe, info, eb):
    whole = lambda shape: pl.BlockSpec(shape, lambda i, *_: (0,) * len(shape))
    return pl.pallas_call(
        ladder_kernel,
        name="ladder",
        grid_spec=pltpu.PrefetchScalarGridSpec(
            num_scalar_prefetch=2,
            grid=(5,),
            in_specs=[
                whole((1600, WIDE)), whole((2, PIECES * PIECE, WIDE)), whole((640, 1024)),
                whole((640, 1024)), whole((64, 128)), whole((8, 1024)),
            ],
            out_specs=pl.BlockSpec((5, 50, 1024), lambda i, *_: (i, 0, 0)),
            scratch_shapes=[
                pltpu.VMEM((640, WIDE), F32),
                pltpu.VMEM((1600, 2 * WIDE), F32),
                pltpu.VMEM((4, 2 * WIDE, 1024), BF),
                pltpu.VMEM((320, 1024), F32),
            ],
        ),
        out_shape=jax.ShapeDtypeStruct((25, 50, 1024), BF),
        compiler_params=pltpu.CompilerParams(vmem_limit_bytes=48 << 20),
    )(info, eb, c, r.reshape(2, PIECES * PIECE, WIDE), t, ts, ea, pe)


def per_device(integrals, amplitudes, virt_irrep, pair_irrep, virt_energy, occ_energy):
    g = jnp.transpose(integrals, (1, 0, 2))
    source = np.arange(1024)
    target = source % 32 * 32 + source // 32
    swap = jnp.asarray((source[:, None] == target[None, :]).astype(jnp.bfloat16))
    t, ts, c, r, ea, pe, info, eb = exchange(
        g, amplitudes.T, virt_irrep, pair_irrep, virt_energy, occ_energy, swap
    )

    def short(_):
        return ladder(t, ts, c, r, ea, pe, info, eb)

    def general(_):
        return jnp.transpose(
            long_runs(integrals, amplitudes, virt_irrep, pair_irrep, virt_energy, occ_energy),
            (1, 0, 2),
        )

    out = lax.cond(info[0] == 1, short, general, 0)
    return jnp.transpose(out, (1, 0, 2))


def solution(mesh):
    return jax.shard_map(
        per_device,
        mesh=mesh,
        in_specs=(P("row", "col", None), P("row", "col"), P(), P(), P(), P()),
        out_specs=P("row", "col", None),
        check_vma=False,
    )
```

```python
import functools

import jax
import jax.numpy as jnp
import numpy as np
from jax import lax
from jax.experimental import pallas as pl
from jax.experimental.pallas import tpu as pltpu
from jax.sharding import PartitionSpec as P

MESH = pl.DeviceIdType.MESH
BF = jnp.bfloat16
F32 = jnp.float32
I32 = jnp.int32
WIDE = 128
RUN = 96
PIECES = 6
PIECE = 80
SPREAD = 8


def pair_swapper(occupied):
    pairs = occupied * occupied
    source = jnp.arange(pairs, dtype=jnp.int32)
    target = source % occupied * occupied + source // occupied
    return (source[:, None] == target[None, :]).astype(jnp.bfloat16)


def long_runs(integrals, amplitudes, virt_irrep, pair_irrep, virt_energy, occ_energy):
    tile_a, tile_b, slab = integrals.shape
    occupied = occ_energy.shape[0]
    pairs = occupied * occupied
    row_at = lax.axis_index("row")
    col_at = lax.axis_index("col")
    labels_a = lax.dynamic_slice_in_dim(virt_irrep, row_at * tile_a, tile_a, 0)
    labels_b = lax.dynamic_slice_in_dim(virt_irrep, col_at * tile_b, tile_b, 0)
    keep = (
        jnp.bitwise_xor(labels_a[:, None, None], labels_b[None, :, None])
        == pair_irrep[None, None, :]
    )
    masked = jnp.where(keep, integrals, jnp.zeros((), integrals.dtype))
    flat = masked.reshape(tile_a * tile_b, slab)
    swapper = pair_swapper(occupied)
    all_pairs = lax.all_gather(amplitudes, "row", axis=0, tiled=True)
    totals = lax.dot_general(
        flat,
        lax.all_gather(all_pairs, "col", axis=1, tiled=True),
        (((1,), (1,)), ((), ())),
        preferred_element_type=jnp.float32,
    )
    rounded = totals.astype(jnp.bfloat16)
    ladder = rounded.reshape(tile_a, tile_b, pairs)
    first_move = lax.all_to_all(ladder, "row", split_axis=2, concat_axis=0, tiled=True)
    second_move = lax.all_to_all(first_move, "col", split_axis=0, concat_axis=1, tiled=True)
    third_move = lax.all_to_all(second_move, "row", split_axis=1, concat_axis=2, tiled=True)
    other = jnp.einsum("bap,pq->abq", third_move, swapper, preferred_element_type=jnp.float32)
    energy_a = lax.dynamic_slice_in_dim(virt_energy, row_at * tile_a, tile_a, 0)
    energy_b = lax.dynamic_slice_in_dim(virt_energy, col_at * tile_b, tile_b, 0)
    pair_energy = (occ_energy[:, None] + occ_energy[None, :]).reshape(pairs)
    denom = energy_a[:, None, None] + energy_b[None, :, None] - pair_energy[None, None, :]
    return ((ladder.astype(jnp.float32) + other) / denom).astype(jnp.bfloat16)


def chip_at(x, y, z, core):
    return (
        y * 2 + lax.div(x, 2),
        lax.rem(x, 2) * 16 + z * 2 + core,
    )


def mirror_chip(x, y, z):
    return (
        lax.rem(z, 2) * 2 + lax.div(y, 4),
        lax.rem(x, 2) * 4 + lax.div(z, 2),
        lax.rem(y, 4) * 2 + lax.div(x, 2),
    )


def exchange_kernel(
    virt_ref, energy_ref, occ_ref, pair_ref, amp_ref, g_ref, swap_ref,
    t_out, ts_out, c_out, r_out, ea_out, pe_out, info_ref, eb_ref,
    gbuf, mbuf, stbuf, swapbuf, cf, cbuf, sendf, sbuf, mid, blocks, tbuf, tile, tfull, tswap, eabuf, pebuf,
    load_sem, swap_sem, out_sem, keep_sem,
    s0_send, s0_recv, s1_send, s1_recv, ring_send, ring_recv, sib_send, sib_recv,
    m1_send, m1_recv, m2_send, m2_recv,
):
    row = lax.axis_index("row")
    col = lax.axis_index("col")
    y, xh = lax.div(row, 2), lax.rem(row, 2)
    xl, core = lax.div(col, 16), lax.rem(col, 2)
    z = lax.div(lax.rem(col, 16), 2)
    x = xh * 2 + xl
    zq, z0 = lax.div(z, 2), lax.rem(z, 2)
    straight = core == xl

    load = pltpu.make_async_copy(g_ref, gbuf, load_sem)
    load.start()
    load_swap = pltpu.make_async_copy(swap_ref, swapbuf, swap_sem)
    load_swap.start()

    def remote(src, dst, send, recv, where):
        return pltpu.make_async_remote_copy(
            src_ref=src, dst_ref=dst, send_sem=send, recv_sem=recv,
            device_id=where, device_id_type=MESH,
        )

    def near(d):
        return chip_at(
            lax.rem(x + 2 * (d // 4), 4), y,
            zq * 2 + lax.rem(z0 + (d // 2) % 2, 2), lax.rem(core + d % 2, 2),
        )

    s1_x = jnp.where(straight, x, xh * 2 + 1 - xl)

    def plane(d):
        return chip_at(s1_x, y, lax.rem(z + 2 * d, 8), xl)

    up = chip_at(x, lax.rem(y + 1, 8), z, core)
    down = chip_at(x, lax.rem(y + 7, 8), z, core)
    sibling = chip_at(x, y, z, 1 - core)
    mx, my, mz = mirror_chip(x, y, z)

    def detour(k, h, t):
        return lax.rem(4 * k + PIECES * h + t, SPREAD)

    def ahead(d):
        return lax.rem(x + d + 1, 4), y, lax.rem(z + d, 8)

    def behind(d):
        return lax.rem(x + 11 - d, 4), y, lax.rem(z + 8 - d, 8)

    def beside_mirror(d):
        return lax.rem(mx + d + 1, 4), my, lax.rem(mz + d, 8)

    def is_here(chip, k):
        return (chip[0] == x) & (chip[1] == y) & (chip[2] == z) & (k == core)

    slots = [(h, t) for t in range(PIECES) for h in range(2)]
    targets = {(h, t): mirror_chip(*behind(detour(core, h, t))) for h, t in slots}
    feeders = {(k, t): beside_mirror(detour(k, core, t)) for k, t in slots}

    barrier = pltpu.get_barrier_semaphore()

    def greet(where):
        pl.semaphore_signal(barrier, inc=1, device_id=where, device_id_type=MESH)

    for k, t in slots:
        @pl.when(jnp.logical_not(is_here(feeders[k, t], k)))
        def _():
            greet(chip_at(*feeders[k, t], k))
    for d in range(SPREAD):
        greet(chip_at(*behind(d), core))
    for d in range(1, 4):
        greet(plane(d))

    @pl.when(jnp.logical_not(straight))
    def _():
        greet(plane(0))

    greet(up)
    greet(down)
    for d in range(1, 8):
        greet(near(d))

    a_at, b_at = row * 50, col * 25
    la0, la1 = virt_ref[a_at], virt_ref[a_at + 49]
    lb0, lb1 = virt_ref[b_at], virt_ref[b_at + 24]
    sa = lax.fori_loop(0, 50, lambda i, n: n + jnp.where(virt_ref[a_at + i] == la0, 1, 0), jnp.int32(0))
    sb = lax.fori_loop(0, 25, lambda i, n: n + jnp.where(virt_ref[b_at + i] == lb0, 1, 0), jnp.int32(0))

    slab = pair_ref.shape[0]
    pair = pair_ref[...].reshape(1, slab)
    starts = [jnp.int32(0)]
    for g in range(1, 8):
        starts.append(jnp.sum(jnp.where(pair < g, 1.0, 0.0)).astype(I32))
    ends = starts[1:] + [jnp.int32(slab)]
    base_of = jnp.zeros_like(pair)
    fits = jnp.int32(1)
    for g in range(8):
        base_of = jnp.where(pair >= g, starts[g], base_of)
        fits = jnp.where(ends[g] - starts[g] > RUN, 0, fits)
    slot_of = lax.broadcasted_iota(I32, pair.shape, 1) - base_of
    stbuf[...] = jnp.where(
        lax.broadcasted_iota(I32, (WIDE, slab), 0) == slot_of, 1.0, 0.0
    ).astype(BF)

    info_ref[0] = fits
    info_ref[1] = sa
    info_ref[2] = sb
    for ja, la in enumerate((la0, la1)):
        for jb, lb in enumerate((lb0, lb1)):
            label = la ^ lb
            start = jnp.int32(0)
            for g in range(1, 8):
                start = jnp.where(label == g, starts[g], start)
            info_ref[4 + 2 * ja + jb] = start

    amp = amp_ref[...].astype(F32)
    packed = jnp.concatenate([amp[0:10], amp[10:20]], axis=1)
    packed = jnp.concatenate([packed, jnp.zeros((6, 128), F32)], axis=0).astype(BF)
    mine = xh * 4 + z0 * 2 + core
    blocks[mine] = packed

    mbuf[...] = jnp.zeros_like(mbuf)
    load.wait()
    first_part = lax.broadcasted_iota(I32, (50, slab), 0) < sa

    def squeeze(i, carry):
        for bb in range(5):
            b = i * 5 + bb
            lb = jnp.where(b < sb, lb0, lb1)
            label = jnp.where(first_part, la0 ^ lb, la1 ^ lb)
            tile = gbuf[b].astype(F32)
            mbuf[bb, 0:50, :] = jnp.where(label == pair, tile, 0.0).astype(BF)
        short = lax.dot_general(
            mbuf[...].reshape(320, slab), stbuf[...], (((1,), (1,)), ((), ())),
            preferred_element_type=F32,
        )
        at = pl.multiple_of(i * 320, 320)
        cf[pl.ds(at, 320), :] = short
        cbuf[pl.ds(at, 320), :] = short.astype(BF)
        return carry

    lax.fori_loop(0, 5, squeeze, 0)
    for h in range(2):
        sendf[h, 624:640, :] = jnp.zeros((16, 128), F32)
        for i in range(25):
            sendf[h, 25 * i:25 * i + 25, :] = cf[pl.ds(25 * h + i, 25, stride=64), :]
        quarter = [sendf[h, 160 * i:160 * i + 160, :] for i in range(4)]
        turned = [pltpu.roll(quarter[i], WIDE - 32 * i, 1) for i in range(1, 4)]
        lane = lax.broadcasted_iota(I32, (160, WIDE), 1)
        sheets = [
            jnp.where(lane < 96, quarter[0], turned[0]),
            jnp.where(lane < 64, turned[0], turned[1]),
            jnp.where(lane < 32, turned[1], turned[2]),
        ]
        for i in range(3):
            sbuf[h, 2 * i:2 * i + 2] = sheets[i].astype(BF).reshape(2, PIECE, WIDE)

    lane8 = lax.broadcasted_iota(I32, (8, 1024), 1)
    first, second = lax.div(lane8, 32), lax.rem(lane8, 32)
    pe = jnp.zeros((8, 1024), F32)
    for i in range(32):
        pe = pe + jnp.where(first == i, occ_ref[i], 0.0) + jnp.where(second == i, occ_ref[i], 0.0)
    pebuf[...] = pe
    sub = lax.broadcasted_iota(I32, (64, 128), 0)
    ea = jnp.ones((64, 128), F32)
    for i in range(50):
        ea = jnp.where(sub == i, energy_ref[a_at + i], ea)
    eabuf[...] = ea

    def copy_eb(i, carry):
        eb_ref[i] = energy_ref[b_at + i]
        return carry

    lax.fori_loop(0, 25, copy_eb, 0)

    expected = jnp.where(straight, SPREAD + 3 + 2 + 7, SPREAD + 4 + 2 + 7)
    for h, t in slots:
        expected = expected + jnp.where(is_here(targets[h, t], h), 0, 1)
    pl.semaphore_wait(barrier, expected)

    outs = (
        pltpu.make_async_copy(cbuf, c_out, out_sem.at[2, 0]),
        pltpu.make_async_copy(eabuf, ea_out, out_sem.at[2, 1]),
        pltpu.make_async_copy(pebuf, pe_out, out_sem.at[3, 0]),
    )
    near_copies = [
        remote(blocks.at[mine], blocks.at[mine], s0_send.at[d - 1], s0_recv.at[mine], near(d))
        for d in range(1, 8)
    ]
    for copy in near_copies:
        copy.start()

    def leg1(h, t):
        return remote(
            sbuf.at[h, t], mid.at[h, t], m1_send.at[h, t], m1_recv.at[h, t],
            chip_at(*ahead(detour(core, h, t)), core),
        )

    def leg2(h, t):
        return remote(
            mid.at[h, t], r_out.at[core, t], m2_send.at[h, t], m2_recv.at[core, t],
            chip_at(*targets[h, t], h),
        )

    def keep_copy(h, t):
        return pltpu.make_async_copy(mid.at[h, t], r_out.at[core, t], keep_sem.at[h, t])

    def forward(h, t):
        leg1(h, t).wait_recv()
        here = is_here(targets[h, t], h)

        @pl.when(jnp.logical_not(here))
        def _():
            leg2(h, t).start()

        @pl.when(here)
        def _():
            keep_copy(h, t).start()

    def near_arrived(s):
        @pl.when(s != mine)
        def _():
            remote(blocks.at[s], blocks.at[s], s0_send.at[0], s0_recv.at[s], sibling).wait_recv()

    for s in range(8):
        near_arrived(s)
    left = lax.broadcasted_iota(I32, (10, 128), 1) < 64
    for q in range(4):
        lo = blocks[q].astype(F32)[0:10]
        hi = blocks[4 + q].astype(F32)[0:10]
        tbuf[20 * q:20 * q + 10, :] = jnp.where(left, lo, pltpu.roll(hi, 64, 1))
        tbuf[20 * q + 10:20 * q + 20, :] = jnp.where(left, pltpu.roll(lo, 64, 1), hi)

    def part(half, quarter, yy):
        at = pl.multiple_of(half * 320 + quarter * 80, 80)
        return tfull.at[pl.ds(at, 80), pl.ds(pl.multiple_of(yy * 128, 128), 128)]

    own_at = pl.multiple_of(xl * 320 + zq * 80, 80)
    lane_at = pl.multiple_of(y * 128, 128)
    tile[...] = tbuf[...].astype(BF)

    @pl.when(straight)
    def _():
        tfull[pl.ds(own_at, 80), pl.ds(lane_at, 128)] = tile[...]

    def spread(d):
        return remote(
            tile, part(xl, zq, y), s1_send.at[d], s1_recv.at[d], plane(d)
        )

    @pl.when(jnp.logical_not(straight))
    def _():
        spread(0).start()

    for d in (1, 3, 2):
        spread(d).start()

    def ring(d, away, sign):
        block = part(core, lax.rem(zq + 4 - d, 4), lax.rem(y + 8 - away * sign, 8))
        index = away if sign > 0 else 8 - away
        return index, block

    def ring_copy(d, step, sign):
        _, block = ring(d, step - 1, sign)
        slot = 2 * step + (sign > 0) - 2
        return remote(
            block, block, ring_send.at[d, slot], ring_recv.at[d, slot],
            up if sign > 0 else down,
        )

    def last_step(d, sign):
        return 4 if (sign > 0) == (d < 2) else 3

    def to_sibling(away, sign):
        yy = lax.rem(y + 8 - away * sign, 8)
        rows = pl.ds(pl.multiple_of(core * 320, 320), 320)
        block = tfull.at[rows, pl.ds(pl.multiple_of(yy * 128, 128), 128)]
        slot = away if sign > 0 else 8 - away
        return remote(block, block, sib_send.at[slot], sib_recv.at[slot], sibling)

    order = (0, 1, 3, 2)
    for d in order:
        if d == 0:
            @pl.when(jnp.logical_not(straight))
            def _():
                spread(0).wait_recv()
        else:
            spread(d).wait_recv()
        for sign in (1, -1):
            ring_copy(d, 1, sign).start()
    to_sibling(0, 1).start()

    def around(step):
        for d in order:
            for sign in (1, -1):
                if step <= last_step(d, sign):
                    ring_copy(d, step, sign).wait_recv()
                    if step + 1 <= last_step(d, sign):
                        ring_copy(d, step + 1, sign).start()
        for sign in (1, -1):
            if step < 4 or sign > 0:
                to_sibling(step, sign).start()

    def deliver(ts):
        for t in ts:
            for h in range(2):
                forward(h, t)

    for h, t in slots:
        leg1(h, t).start()

    for copy in outs:
        copy.start()
    around(1)
    around(2)
    deliver((0, 1, 2))
    around(3)
    deliver((3, 4, 5))
    around(4)

    load_swap.wait()

    def rows_out(half):
        rows = pl.ds(pl.multiple_of(half * 320, 320), 320)
        return (
            pltpu.make_async_copy(tfull.at[rows], t_out.at[rows], out_sem.at[0, half]),
            pltpu.make_async_copy(tswap.at[rows], ts_out.at[rows], out_sem.at[1, half]),
        )

    def swapped(half):
        rows = pl.ds(pl.multiple_of(half * 320, 320), 320)
        plain, turned = rows_out(half)
        plain.start()

        def block(i, carry):
            at = pl.ds(pl.multiple_of(half * 320 + i * 64, 64), 64)
            tswap[at, :] = jnp.dot(tfull[at, :], swapbuf[...], preferred_element_type=F32).astype(BF)
            return carry

        lax.fori_loop(0, 5, block, 0)
        turned.start()

    swapped(core)
    for slot in range(8):
        step = slot if slot <= 4 else 8 - slot
        to_sibling(step, 1 if slot <= 4 else -1).wait_recv()
    swapped(1 - core)
    for k, t in slots:
        @pl.when(jnp.logical_not(is_here(feeders[k, t], k)))
        def _():
            remote(
                mid.at[0, t], r_out.at[k, t], m2_send.at[0, t], m2_recv.at[k, t], sibling
            ).wait_recv()
    for h, t in slots:
        here = is_here(targets[h, t], h)

        @pl.when(here)
        def _():
            keep_copy(h, t).wait()

        @pl.when(jnp.logical_not(here))
        def _():
            leg2(h, t).wait_send()

        leg1(h, t).wait_send()
    for copy in near_copies:
        copy.wait_send()

    @pl.when(jnp.logical_not(straight))
    def _():
        spread(0).wait_send()

    for d in (1, 3, 2):
        spread(d).wait_send()
    for d in range(4):
        for sign in (1, -1):
            for step in range(1, last_step(d, sign) + 1):
                ring_copy(d, step, sign).wait_send()
    for slot in range(8):
        step = slot if slot <= 4 else 8 - slot
        to_sibling(step, 1 if slot <= 4 else -1).wait_send()
    for copy in outs + rows_out(core) + rows_out(1 - core):
        copy.wait()


def exchange(g, amp, virt_irrep, pair_irrep, virt_energy, occ_energy, swap):
    dma, vmem = pltpu.SemaphoreType.DMA, pltpu.VMEM
    smem_spec = pl.BlockSpec(memory_space=pltpu.SMEM)
    vmem_spec = pl.BlockSpec(memory_space=pltpu.VMEM)
    any_spec = pl.BlockSpec(memory_space=pl.ANY)
    return pl.pallas_call(
        exchange_kernel,
        name="exchange",
        out_shape=[
            jax.ShapeDtypeStruct((640, 1024), BF),
            jax.ShapeDtypeStruct((640, 1024), BF),
            jax.ShapeDtypeStruct((1600, WIDE), BF),
            jax.ShapeDtypeStruct((2, PIECES, PIECE, WIDE), BF),
            jax.ShapeDtypeStruct((64, 128), F32),
            jax.ShapeDtypeStruct((8, 1024), F32),
            jax.ShapeDtypeStruct((8,), I32),
            jax.ShapeDtypeStruct((32,), F32),
        ],
        in_specs=[smem_spec, smem_spec, smem_spec, vmem_spec, vmem_spec, any_spec, any_spec],
        out_specs=[any_spec] * 6 + [smem_spec] * 2,
        scratch_shapes=[
            vmem((25, 50, 640), BF),
            vmem((5, 64, 640), BF),
            vmem((WIDE, 640), BF),
            vmem((1024, 1024), BF),
            vmem((1600, WIDE), F32),
            vmem((1600, WIDE), BF),
            vmem((2, 640, WIDE), F32),
            vmem((2, PIECES, PIECE, WIDE), BF),
            vmem((2, PIECES, PIECE, WIDE), BF),
            vmem((8, 16, 128), BF),
            vmem((80, 128), F32),
            vmem((80, 128), BF),
            vmem((640, 1024), BF),
            vmem((640, 1024), BF),
            vmem((64, 128), F32),
            vmem((8, 1024), F32),
            dma, dma, dma((4, 2)), dma((2, PIECES)),
            dma((7,)), dma((8,)), dma((4,)), dma((4,)), dma((4, 8)), dma((4, 8)),
            dma((8,)), dma((8,)),
            dma((2, PIECES)), dma((2, PIECES)), dma((2, PIECES)), dma((2, PIECES)),
        ],
        compiler_params=pltpu.CompilerParams(
            collective_id=1, has_side_effects=True, vmem_limit_bytes=60 << 20
        ),
    )(virt_irrep, virt_energy, occ_energy, pair_irrep, amp, g, swap)


def ladder_kernel(info, eb, c_ref, r_ref, t_ref, ts_ref, ea_ref, pe_ref, out_ref, messf, xall, rhs, acc):
    step = pl.program_id(0)
    sa, sb = info[1], info[2]
    two_a = sa < 50
    two_b = sb < 25

    def base_of(ja, jb):
        start = info[4 + 2 * ja + jb]
        return pl.multiple_of(jnp.minimum(lax.div(start, 16) * 16, t_ref.shape[0] - WIDE), 16)

    @pl.when(step == 0)
    def _():
        lane = lax.broadcasted_iota(I32, (160, WIDE), 1)
        xall[:, 0:WIDE] = c_ref[...].astype(F32)
        xall[:, WIDE:2 * WIDE] = jnp.zeros((1600, WIDE), F32)
        for k in range(2):
            sheets = [r_ref[k, 160 * i:160 * i + 160, :].astype(F32) for i in range(3)]
            messf[0:160, :] = jnp.where(lane < 96, sheets[0], 0.0)
            for i in range(1, 4):
                low = sheets[i] if i < 3 else jnp.zeros((160, WIDE), F32)
                both = jnp.where(
                    lane >= WIDE - 32 * i, sheets[i - 1], jnp.where(lane < 96 - 32 * i, low, 0.0)
                )
                messf[160 * i:160 * i + 160, :] = pltpu.roll(both, 32 * i, 1)
            for b in range(25):
                xall[64 * b + 25 * k:64 * b + 25 * k + 25, WIDE:2 * WIDE] = messf[25 * b:25 * b + 25, :]
        for ja in range(2):
            for jb in range(2):
                def fill(ja=ja, jb=jb):
                    rows = pl.ds(base_of(ja, jb), WIDE)
                    rhs[2 * ja + jb, 0:WIDE, :] = t_ref[rows, :]
                    rhs[2 * ja + jb, WIDE:2 * WIDE, :] = ts_ref[rows, :]

                needed = True if ja + jb == 0 else (two_a if jb == 0 else two_b if ja == 0 else two_a & two_b)
                if needed is True:
                    fill()
                else:
                    pl.when(needed)(fill)

    b0 = step * 5
    at = pl.multiple_of(step * 320, 320)
    place = lax.broadcasted_iota(I32, (320, WIDE), 0)
    in_a = lax.rem(place, 64) >= sa
    in_b = b0 + lax.div(place, 64) >= sb

    def product(ja, jb):
        side_a = in_a if ja else jnp.logical_not(in_a)
        side = side_a & (jnp.where(in_b, 1, 0) == jb)
        turn = info[4 + 2 * ja + jb] - base_of(ja, jb)
        lhs = jnp.concatenate([
            jnp.where(side, pltpu.roll(xall[pl.ds(at, 320), WIDE * i:WIDE * i + WIDE], turn, 1), 0.0).astype(BF)
            for i in range(2)
        ], axis=1)
        return jnp.dot(lhs, rhs[2 * ja + jb], preferred_element_type=F32)

    lead = jnp.where(b0 >= sb, 1, 0)
    straddle = (b0 < sb) & (b0 + 5 > sb)
    acc[...] = product(0, lead)

    @pl.when(two_a)
    def _():
        acc[...] += product(1, lead)

    @pl.when(straddle)
    def _():
        acc[...] += product(0, 1)

    @pl.when(straddle & two_a)
    def _():
        acc[...] += product(1, 1)

    pe = pe_ref[0:1, :]
    for bb in range(5):
        ea = ea_ref[0:50, 0:1] + eb[b0 + bb]
        out_ref[bb] = (acc[64 * bb:64 * bb + 50, :] / (ea - pe)).astype(BF)


def ladder(t, ts, c, r, ea, pe, info, eb):
    whole = lambda shape: pl.BlockSpec(shape, lambda i, *_: (0,) * len(shape))
    return pl.pallas_call(
        ladder_kernel,
        name="ladder",
        grid_spec=pltpu.PrefetchScalarGridSpec(
            num_scalar_prefetch=2,
            grid=(5,),
            in_specs=[
                whole((1600, WIDE)), whole((2, PIECES * PIECE, WIDE)), whole((640, 1024)),
                whole((640, 1024)), whole((64, 128)), whole((8, 1024)),
            ],
            out_specs=pl.BlockSpec((5, 50, 1024), lambda i, *_: (i, 0, 0)),
            scratch_shapes=[
                pltpu.VMEM((640, WIDE), F32),
                pltpu.VMEM((1600, 2 * WIDE), F32),
                pltpu.VMEM((4, 2 * WIDE, 1024), BF),
                pltpu.VMEM((320, 1024), F32),
            ],
        ),
        out_shape=jax.ShapeDtypeStruct((25, 50, 1024), BF),
        compiler_params=pltpu.CompilerParams(vmem_limit_bytes=48 << 20),
    )(info, eb, c, r.reshape(2, PIECES * PIECE, WIDE), t, ts, ea, pe)


def per_device(integrals, amplitudes, virt_irrep, pair_irrep, virt_energy, occ_energy):
    g = jnp.transpose(integrals, (1, 0, 2))
    source = np.arange(1024)
    target = source % 32 * 32 + source // 32
    swap = jnp.asarray((source[:, None] == target[None, :]).astype(jnp.bfloat16))
    t, ts, c, r, ea, pe, info, eb = exchange(
        g, amplitudes.T, virt_irrep, pair_irrep, virt_energy, occ_energy, swap
    )

    def short(_):
        return ladder(t, ts, c, r, ea, pe, info, eb)

    def general(_):
        return jnp.transpose(
            long_runs(integrals, amplitudes, virt_irrep, pair_irrep, virt_energy, occ_energy),
            (1, 0, 2),
        )

    out = lax.cond(info[0] == 1, short, general, 0)
    return jnp.transpose(out, (1, 0, 2))


def solution(mesh):
    return jax.shard_map(
        per_device,
        mesh=mesh,
        in_specs=(P("row", "col", None), P("row", "col"), P(), P(), P(), P()),
        out_specs=P("row", "col", None),
        check_vma=False,
    )
```
